32 devices in a mesh: row: 8 (over y, x, core), col: 4 (over z).
Axes of the slice: x: 2, y: 2, z: 4, core: 2. Of those that a mesh axis runs over, the one named last changes fastest.
Arguments:
- density: float32 [1024, 1024], P('row', 'col'), as said below
- pattern: int32 [16, 16], P('row', 'col'), may hold values from 0 to 1, as said below
Outputs:
- purified: float32 [1024, 1024], P('row', 'col')
The draws below stay inside these ranges and needn't reach their ends.
Inputs may be any that keep to these rules, and one draw needn't show every extreme that they name: pattern is symmetric and its diagonal is 1. density is symmetric and zero in every block where pattern is 0.
All inputs are finite; a program needn't handle non-finite values.
Results may differ from the reference program's by a relative error of at most 0.00013.
Values sent between devices are 32-bit elements; how exact they have to be, the bound alone decides.
A program may use at most 64 MiB of HBM per device.

```python
import jax
import jax.numpy as jnp
from jax import lax

BLK = 64
ITERS = 2
NB = 16


def pattern_bits(key):
    base_key = jax.random.fold_in(key, 7)
    raw_bits = jax.random.randint(base_key, (NB, NB), 0, 4)
    chosen = (raw_bits == 0).astype(jnp.int32)
    mirrored = jnp.maximum(chosen, chosen.T)
    identity = (jnp.arange(NB)[:, None] == jnp.arange(NB)[None, :]).astype(jnp.int32)
    return jnp.maximum(mirrored, identity)


def draw_pattern(key, part):
    return pattern_bits(key)


def draw_density(key, part):
    kept = pattern_bits(key).astype(jnp.float32)
    widened = jnp.repeat(jnp.repeat(kept, BLK, axis=0), BLK, axis=1)
    spread_scale = 0.5 / jnp.sqrt(jnp.float32(NB * BLK))
    first_key = jax.random.fold_in(key, 11)
    second_key = jax.random.fold_in(key, 13)
    values = jax.random.normal(first_key, (NB * BLK, NB * BLK), jnp.float32)
    diagonal_values = jax.random.uniform(second_key, (NB * BLK,), jnp.float32, 0.2, 0.8)
    symmetric = (values + values.T) * 0.70710678 * spread_scale
    on_diagonal = (jnp.arange(NB * BLK)[:, None] == jnp.arange(NB * BLK)[None, :]).astype(jnp.float32)
    result = widened * symmetric * (1.0 - on_diagonal) + on_diagonal * diagonal_values[:, None]
    return result.astype(jnp.float32)


def setup_inputs(seed: int = 0) -> dict:
    keys = jax.random.split(jax.random.key(seed), 3)
    return {
        "density": draw_density(jax.random.fold_in(keys[2], 71), 0),
        "pattern": draw_pattern(jax.random.fold_in(keys[2], 71), 0),
    }


def expand_mask(pattern):
    widened = jnp.repeat(jnp.repeat(pattern, BLK, axis=0), BLK, axis=1)
    return widened.astype(jnp.float32)


def reference(density, pattern):
    block_mask = expand_mask(pattern)
    current = density
    for step in range(ITERS):
        square = block_mask * jnp.dot(current, current, precision=lax.Precision.HIGHEST, preferred_element_type=jnp.float32)
        cube = block_mask * jnp.dot(square, current, precision=lax.Precision.HIGHEST, preferred_element_type=jnp.float32)
        current = 3.0 * square - 2.0 * cube
    return current
```

```python
import functools

import jax
import jax.numpy as jnp
from jax import lax
from jax.experimental import pallas as pl
from jax.experimental.pallas import tpu as pltpu
from jax.sharding import PartitionSpec as P

ITERS = 2
MESH = pl.DeviceIdType.MESH


def split(x):
    high = x.astype(jnp.bfloat16)
    low = (x - high.astype(jnp.float32)).astype(jnp.bfloat16)
    return high, low


def flip(index, mask):
    bit = 1
    while bit <= mask:
        if mask & bit:
            index = index + bit * (1 - 2 * lax.rem(index // bit, 2))
        bit *= 2
    return index


def kernel(nrow, ncol, pattern_ref, density_ref, out_ref, rowp, cols, srow, bh, bl, acc, mask,
           zs, zr, cs, cr, ss, sr):
    h, w = density_ref.shape
    pr, pc = pattern_ref.shape
    plane = nrow // 2
    r, z = lax.axis_index("row"), lax.axis_index("col")
    core = lax.rem(r, 2)
    chip = r // 2
    sib = r + 1 - 2 * core
    zright, zleft = lax.rem(z + 1, ncol), lax.rem(z + ncol - 1, ncol)

    barrier = pltpu.get_barrier_semaphore()
    greet = [(flip(chip, d) * 2 + core, z) for d in range(1, plane)]
    greet += [(sib, z), (r, zright), (r, zleft)]
    for device in greet:
        pl.semaphore_signal(barrier, inc=1, device_id=device, device_id_type=MESH)

    lane_block = lax.broadcasted_iota(jnp.int32, (h // pr, w), 1) // (w // pc)
    for i in range(pr):
        band = jnp.zeros((h // pr, w), jnp.float32)
        for j in range(pc):
            band = jnp.where(lane_block == j, pattern_ref[i, j].astype(jnp.float32), band)
        mask[i * (h // pr):(i + 1) * (h // pr), :] = band

    def rows_of(owner):
        return pl.ds(pl.multiple_of(owner * h, h), h)

    rowp[0, z] = density_ref[...]
    cols[0, rows_of(r), :] = density_ref[...]
    pl.semaphore_wait(barrier, len(greet))

    def remote(ref, send, recv, device):
        return pltpu.make_async_remote_copy(
            src_ref=ref, dst_ref=ref, send_sem=send, recv_sem=recv, device_id=device, device_id_type=MESH)

    def zcopy(buf, ph, way, s, j):
        return remote(buf.at[j], zs.at[ph, way, s], zr.at[ph, way, s], (r, zright if way == 0 else zleft))

    def zstart(buf, ph):
        @pl.when(z < ncol - 1)
        def _():
            zcopy(buf, ph, 0, 0, z).start()

        @pl.when(z > 0)
        def _():
            zcopy(buf, ph, 1, 0, z).start()

    def arrive(buf, ph, s):
        @pl.when(z - s >= 0)
        def _():
            zcopy(buf, ph, 0, s - 1, z - s).wait_recv()

            @pl.when(z < ncol - 1)
            def _():
                zcopy(buf, ph, 0, s, z - s).start()

        @pl.when(z + s <= ncol - 1)
        def _():
            zcopy(buf, ph, 1, s - 1, z + s).wait_recv()

            @pl.when(z > 0)
            def _():
                zcopy(buf, ph, 1, s, z + s).start()

    def zfinish(buf, ph):
        def one(s):
            @pl.when((z - s >= 0) & (z < ncol - 1))
            def _():
                zcopy(buf, ph, 0, s, z - s).wait_send()

            @pl.when((z + s <= ncol - 1) & (z > 0))
            def _():
                zcopy(buf, ph, 1, s, z + s).wait_send()

        over(0, ncol - 1, one)

    def over(low, high, body):
        if ncol <= 4:
            for s in range(low, high):
                body(s)
        else:
            lax.fori_loop(low, high, lambda s, c: (body(s), c)[1], 0)

    def colcopy(it, d, owner, device):
        return remote(cols.at[it, rows_of(owner)], cs.at[it, d], cr.at[it, d], (device, z))

    def sibcopy(it, d, owner):
        return remote(cols.at[it, rows_of(owner)], ss.at[it, d], sr.at[it, d], (sib, z))

    def chunk(buf, it, j, fresh):
        rows = pl.ds(pl.multiple_of(j * w, w), w)
        if fresh:
            bhigh, blow = split(cols[it, rows, :])
            bh[rows, :] = bhigh
            bl[rows, :] = blow
        else:
            bhigh, blow = bh[rows, :], bl[rows, :]
        ahigh, alow = split(buf[j])
        both = jnp.concatenate([ahigh, alow], axis=0)
        p = jnp.dot(both, bhigh, preferred_element_type=jnp.float32)
        q = jnp.dot(ahigh, blow, preferred_element_type=jnp.float32)
        acc[...] += p[:h] + (p[h:] + q)

    def compute(buf, it, s, fresh):
        @pl.when(z - s >= 0)
        def _():
            chunk(buf, it, z - s, fresh)

        @pl.when(z + s <= ncol - 1)
        def _():
            chunk(buf, it, z + s, fresh)

    for it in range(ITERS):
        cur, sq = rowp.at[it], srow.at[it]
        pa, pb = 2 * it, 2 * it + 1
        zstart(cur, pa)
        for d in range(1, plane):
            colcopy(it, d, r, flip(chip, d) * 2 + core).start()
        sibcopy(it, 0, r).start()
        acc[...] = jnp.zeros_like(acc)
        arrive(cur, pa, 1)
        for d in range(1, plane):
            peer = flip(chip, d) * 2 + core
            colcopy(it, d, peer, peer).wait_recv()
            sibcopy(it, d, peer).start()
        arrive(cur, pa, 2)
        for d in range(plane):
            sibcopy(it, d, flip(chip, d) * 2 + 1 - core).wait_recv()
        chunk(cur, it, z, True)
        compute(cur, it, 1, True)
        compute(cur, it, 2, True)

        def finish(s):
            arrive(cur, pa, s)
            compute(cur, it, s, True)

        over(3, ncol, finish)
        square = acc[...] * mask[...]
        sq[z] = square
        zstart(sq, pb)
        acc[...] = jnp.zeros_like(acc)
        chunk(sq, it, z, False)

        def cube(s):
            arrive(sq, pb, s)
            compute(sq, it, s, False)

        over(1, ncol, cube)
        result = 3.0 * sq[z] - 2.0 * (mask[...] * acc[...])
        if it + 1 < ITERS:
            rowp[it + 1, z] = result
            cols[it + 1, rows_of(r), :] = result
        else:
            out_ref[...] = result

    for it in range(ITERS):
        zfinish(rowp.at[it], 2 * it)
        zfinish(srow.at[it], 2 * it + 1)
        for d in range(plane):
            peer = flip(chip, d) * 2 + core
            if d:
                colcopy(it, d, r, peer).wait_send()
            sibcopy(it, d, peer).wait_send()


def solution(mesh):
    nrow, ncol = mesh.shape["row"], mesh.shape["col"]

    def per_device(density, pattern):
        h, w = density.shape
        n = nrow * h
        f32 = jnp.float32
        dma = pltpu.SemaphoreType.DMA
        return pl.pallas_call(
            functools.partial(kernel, nrow, ncol),
            out_shape=jax.ShapeDtypeStruct((h, w), f32),
            in_specs=[pl.BlockSpec(memory_space=pltpu.SMEM), pl.BlockSpec(memory_space=pltpu.VMEM)],
            out_specs=pl.BlockSpec(memory_space=pltpu.VMEM),
            scratch_shapes=[
                pltpu.VMEM((ITERS, ncol, h, w), f32),
                pltpu.VMEM((ITERS, n, w), f32),
                pltpu.VMEM((ITERS, ncol, h, w), f32),
                pltpu.VMEM((n, w), jnp.bfloat16),
                pltpu.VMEM((n, w), jnp.bfloat16),
                pltpu.VMEM((h, w), f32),
                pltpu.VMEM((h, w), f32),
                dma((2 * ITERS, 2, ncol)),
                dma((2 * ITERS, 2, ncol)),
                dma((ITERS, nrow // 2)),
                dma((ITERS, nrow // 2)),
                dma((ITERS, nrow // 2)),
                dma((ITERS, nrow // 2)),
            ],
            compiler_params=pltpu.CompilerParams(
                collective_id=0, has_side_effects=True, vmem_limit_bytes=40 * 1024 * 1024),
            cost_estimate=pl.CostEstimate(
                flops=12 * ITERS * h * n * w, bytes_accessed=8 * h * w, transcendentals=0),
        )(pattern, density)

    return jax.shard_map(
        per_device,
        mesh=mesh,
        in_specs=(P("row", "col"), P("row", "col")),
        out_specs=P("row", "col"),
        check_vma=False,
    )
```

```python
import functools

import jax
import jax.numpy as jnp
from jax import lax
from jax.experimental import pallas as pl
from jax.experimental.pallas import tpu as pltpu
from jax.sharding import PartitionSpec as P

ITERS = 2
PIECES = 2
NEAR = 2
MESH = pl.DeviceIdType.MESH


def split(x):
    high = x.astype(jnp.bfloat16)
    low = (x - high.astype(jnp.float32)).astype(jnp.bfloat16)
    return high, low


def flip(index, mask):
    bit = 1
    while bit <= mask:
        if mask & bit:
            index = index + bit * (1 - 2 * lax.rem(index // bit, 2))
        bit *= 2
    return index


def kernel(nrow, ncol, pattern_ref, density_ref, out_ref, rowp, cols, srow, bh, bl, acc, mask,
           zs, zr, cs, cr, ss, sr):
    h, w = density_ref.shape
    pr, pc = pattern_ref.shape
    plane = nrow // 2
    r, z = lax.axis_index("row"), lax.axis_index("col")
    core = lax.rem(r, 2)
    chip = r // 2
    sib = r + 1 - 2 * core
    hp = h // PIECES

    barrier = pltpu.get_barrier_semaphore()
    hops = sorted({d % ncol for near in range(1, NEAR + 1) for d in (near, -near)} - {0})
    greet = [(flip(chip, d) * 2 + core, z) for d in range(1, plane)] + [(sib, z)]
    greet += [(r, lax.rem(z + d, ncol)) for d in hops]
    for device in greet:
        pl.semaphore_signal(barrier, inc=1, device_id=device, device_id_type=MESH)

    lane_block = lax.broadcasted_iota(jnp.int32, (h // pr, w), 1) // (w // pc)
    for i in range(pr):
        band = jnp.zeros((h // pr, w), jnp.float32)
        for j in range(pc):
            band = jnp.where(lane_block == j, pattern_ref[i, j].astype(jnp.float32), band)
        mask[i * (h // pr):(i + 1) * (h // pr), :] = band

    def rows_of(owner, p):
        return pl.ds(pl.multiple_of(owner * h + p * hp, hp), hp)

    def part(p):
        return pl.ds(p * hp, hp)

    rowp[0, z] = density_ref[...]
    cols[0, pl.ds(pl.multiple_of(r * h, h), h), :] = density_ref[...]
    acc[...] = jnp.zeros_like(acc)
    pl.semaphore_wait(barrier, len(greet))

    def remote(ref, send, recv, device):
        return pltpu.make_async_remote_copy(
            src_ref=ref, dst_ref=ref, send_sem=send, recv_sem=recv, device_id=device, device_id_type=MESH)

    def over(low, high, body):
        if ncol <= 4:
            for s in range(low, high):
                body(s)
        else:
            lax.fori_loop(low, high, lambda s, c: (body(s), c)[1], 0)

    def zsend(buf, ph, p, way, s, act, near):
        sign = 1 - 2 * way
        back = 0 if near else s - 1
        ahead = s if near else 1
        block, to = z - sign * back, z + sign * ahead

        @pl.when((block >= 0) & (block <= ncol - 1) & (to >= 0) & (to <= ncol - 1))
        def _():
            copy = remote(buf.at[block, part(p)], zs.at[ph, p, way, s - 1], zr.at[ph, p, way, s - 1], (r, to))
            copy.start() if act == "start" else copy.wait_send()

    def zown(buf, ph, p):
        for s in range(min(NEAR, ncol - 1), 0, -1):
            for way in (0, 1):
                zsend(buf, ph, p, way, s, "start", True)

    def arrive(buf, ph, p, s, passes):
        for way in (0, 1):
            sign = 1 - 2 * way
            block = z - sign * s

            @pl.when((block >= 0) & (block <= ncol - 1))
            def _():
                remote(buf.at[block, part(p)], zs.at[ph, p, way, s - 1], zr.at[ph, p, way, s - 1],
                       (r, z - sign)).wait_recv()
            if passes:
                zsend(buf, ph, p, way, s + 1, "start", False)

    def colcopy(it, p, d, owner, device):
        return remote(cols.at[it, rows_of(owner, p)], cs.at[it, p, d], cr.at[it, p, d], (device, z))

    def sibcopy(it, p, d, owner):
        return remote(cols.at[it, rows_of(owner, p)], ss.at[it, p, d], sr.at[it, p, d], (sib, z))

    def chunk(buf, it, p, j, fresh):
        rows = pl.ds(pl.multiple_of(j * w, w), w)
        if fresh:
            bhigh, blow = split(cols[it, rows, :])
            bh[rows, :] = bhigh
            bl[rows, :] = blow
        else:
            bhigh, blow = bh[rows, :], bl[rows, :]
        ahigh, alow = split(buf[j, part(p), :])
        both = jnp.concatenate([ahigh, alow], axis=0)
        prod = jnp.dot(both, bhigh, preferred_element_type=jnp.float32)
        rest = jnp.dot(ahigh, blow, preferred_element_type=jnp.float32)
        acc[part(p), :] += prod[:hp] + (prod[hp:] + rest)

    def compute(buf, it, p, s, fresh):
        @pl.when(z - s >= 0)
        def _():
            chunk(buf, it, p, z - s, fresh)

        @pl.when(z + s <= ncol - 1)
        def _():
            chunk(buf, it, p, z + s, fresh)

    def finish(buf, ph, it, p, fresh):
        for s in range(1, min(NEAR, ncol - 1) + 1):
            if s < NEAR:
                arrive(buf, ph, p, s, False)
            compute(buf, it, p, s, fresh)

        def far(s):
            arrive(buf, ph, p, s, True)
            compute(buf, it, p, s, fresh)

        over(NEAR + 1, ncol, far)

    def begin(it, p):
        zown(rowp.at[it], 2 * it, p)
        for d in range(1, plane):
            colcopy(it, p, d, r, flip(chip, d) * 2 + core).start()
        sibcopy(it, p, 0, r).start()

    for p in range(PIECES):
        begin(0, p)
    for it in range(ITERS):
        cur, sq = rowp.at[it], srow.at[it]
        pa, pb = 2 * it, 2 * it + 1
        for p in range(PIECES):
            arrive(cur, pa, p, NEAR, True)
            for d in range(1, plane):
                peer = flip(chip, d) * 2 + core
                colcopy(it, p, d, peer, peer).wait_recv()
                sibcopy(it, p, d, peer).start()
        for p in range(PIECES):
            for d in range(plane):
                sibcopy(it, p, d, flip(chip, d) * 2 + 1 - core).wait_recv()
        for p in range(PIECES):
            chunk(cur, it, p, z, p == 0)
            finish(cur, pa, it, p, p == 0)
            sq[z, part(p), :] = acc[part(p), :] * mask[part(p), :]
            acc[part(p), :] = jnp.zeros((hp, w), jnp.float32)
            zown(sq, pb, p)
        for p in range(PIECES):
            chunk(sq, it, p, z, False)
            arrive(sq, pb, p, NEAR, True)
        for p in range(PIECES):
            finish(sq, pb, it, p, False)
            result = 3.0 * sq[z, part(p), :] - 2.0 * (mask[part(p), :] * acc[part(p), :])
            if it + 1 < ITERS:
                acc[part(p), :] = jnp.zeros((hp, w), jnp.float32)
                rowp[it + 1, z, part(p), :] = result
                cols[it + 1, rows_of(r, p), :] = result
                begin(it + 1, p)
            else:
                out_ref[part(p), :] = result

    for it in range(ITERS):
        for p in range(PIECES):
            for buf, ph in ((rowp.at[it], 2 * it), (srow.at[it], 2 * it + 1)):
                for s in range(1, min(NEAR, ncol - 1) + 1):
                    for way in (0, 1):
                        zsend(buf, ph, p, way, s, "wait", True)

                def sent(s):
                    for way in (0, 1):
                        zsend(buf, ph, p, way, s, "wait", False)

                over(NEAR + 1, ncol, sent)
            for d in range(plane):
                peer = flip(chip, d) * 2 + core
                if d:
                    colcopy(it, p, d, r, peer).wait_send()
                sibcopy(it, p, d, peer).wait_send()


def solution(mesh):
    nrow, ncol = mesh.shape["row"], mesh.shape["col"]

    def per_device(density, pattern):
        h, w = density.shape
        n = nrow * h
        f32 = jnp.float32
        dma = pltpu.SemaphoreType.DMA
        return pl.pallas_call(
            functools.partial(kernel, nrow, ncol),
            out_shape=jax.ShapeDtypeStruct((h, w), f32),
            in_specs=[pl.BlockSpec(memory_space=pltpu.SMEM), pl.BlockSpec(memory_space=pltpu.VMEM)],
            out_specs=pl.BlockSpec(memory_space=pltpu.VMEM),
            scratch_shapes=[
                pltpu.VMEM((ITERS, ncol, h, w), f32),
                pltpu.VMEM((ITERS, n, w), f32),
                pltpu.VMEM((ITERS, ncol, h, w), f32),
                pltpu.VMEM((n, w), jnp.bfloat16),
                pltpu.VMEM((n, w), jnp.bfloat16),
                pltpu.VMEM((h, w), f32),
                pltpu.VMEM((h, w), f32),
                dma((2 * ITERS, PIECES, 2, ncol)),
                dma((2 * ITERS, PIECES, 2, ncol)),
                dma((ITERS, PIECES, nrow // 2)),
                dma((ITERS, PIECES, nrow // 2)),
                dma((ITERS, PIECES, nrow // 2)),
                dma((ITERS, PIECES, nrow // 2)),
            ],
            compiler_params=pltpu.CompilerParams(
                collective_id=0, has_side_effects=True, vmem_limit_bytes=40 * 1024 * 1024),
            cost_estimate=pl.CostEstimate(
                flops=12 * ITERS * h * n * w, bytes_accessed=8 * h * w, transcendentals=0),
        )(pattern, density)

    return jax.shard_map(
        per_device,
        mesh=mesh,
        in_specs=(P("row", "col"), P("row", "col")),
        out_specs=P("row", "col"),
        check_vma=False,
    )
```

```python
import functools

import jax
import jax.numpy as jnp
from jax import lax
from jax.experimental import pallas as pl
from jax.experimental.pallas import tpu as pltpu
from jax.sharding import PartitionSpec as P

ITERS = 2
PIECES = 2
NEAR = 2
MESH = pl.DeviceIdType.MESH


def split(x):
    high = x.astype(jnp.bfloat16)
    low = (x - high.astype(jnp.float32)).astype(jnp.bfloat16)
    return high, low


def flip(index, mask):
    bit = 1
    while bit <= mask:
        if mask & bit:
            index = index + bit * (1 - 2 * lax.rem(index // bit, 2))
        bit *= 2
    return index


def kernel(nrow, ncol, pattern_hbm, density_ref, out_ref, pattern_ref, local, rowp, cols, srow, bh, bl, acc, mask,
           zs, zr, cs, cr, ss, sr):
    h, w = density_ref.shape
    pr, pc = pattern_hbm.shape
    plane = nrow // 2
    r, z = lax.axis_index("row"), lax.axis_index("col")
    core = lax.rem(r, 2)
    chip = r // 2
    sib = r + 1 - 2 * core
    hp = h // PIECES

    take_pattern = pltpu.make_async_copy(pattern_hbm, pattern_ref, local.at[0])
    take_density = pltpu.make_async_copy(density_ref, rowp.at[0, z], local.at[1])
    take_pattern.start()
    take_density.start()
    barrier = pltpu.get_barrier_semaphore()
    hops = sorted({d % ncol for near in range(1, NEAR + 1) for d in (near, -near)} - {0})
    greet = [(flip(chip, d) * 2 + core, z) for d in range(1, plane)] + [(sib, z)]
    greet += [(r, lax.rem(z + d, ncol)) for d in hops]
    for device in greet:
        pl.semaphore_signal(barrier, inc=1, device_id=device, device_id_type=MESH)

    take_pattern.wait()
    lane_block = lax.broadcasted_iota(jnp.int32, (h // pr, w), 1) // (w // pc)
    for i in range(pr):
        band = jnp.zeros((h // pr, w), jnp.float32)
        for j in range(pc):
            band = jnp.where(lane_block == j, pattern_ref[i, j].astype(jnp.float32), band)
        mask[i * (h // pr):(i + 1) * (h // pr), :] = band

    def rows_of(owner, p):
        return pl.ds(pl.multiple_of(owner * h + p * hp, hp), hp)

    def part(p):
        return pl.ds(p * hp, hp)

    take_density.wait()
    cols[0, pl.ds(pl.multiple_of(r * h, h), h), :] = rowp[0, z]
    acc[...] = jnp.zeros_like(acc)
    pl.semaphore_wait(barrier, len(greet))

    def remote(ref, send, recv, device):
        return pltpu.make_async_remote_copy(
            src_ref=ref, dst_ref=ref, send_sem=send, recv_sem=recv, device_id=device, device_id_type=MESH)

    def over(low, high, body):
        if ncol <= 4:
            for s in range(low, high):
                body(s)
        else:
            lax.fori_loop(low, high, lambda s, c: (body(s), c)[1], 0)

    def zsend(buf, ph, p, way, s, act, near, only=None):
        sign = 1 - 2 * way
        back = 0 if near else s - 1
        ahead = s if near else 1
        block, to = z - sign * back, z + sign * ahead

        inside = (block >= 0) & (block <= ncol - 1) & (to >= 0) & (to <= ncol - 1)
        if only == "end":
            inside = (to == (ncol - 1 if way == 0 else 0)) & (block >= 0) & (block <= ncol - 1)
        elif only == "middle":
            inside = (to > 0) & (to < ncol - 1)

        @pl.when(inside)
        def _():
            copy = remote(buf.at[block, part(p)], zs.at[ph, p, way, s - 1], zr.at[ph, p, way, s - 1], (r, to))
            copy.start() if act == "start" else copy.wait_send()

    def zown(buf, ph, p):
        for way in (0, 1):
            zsend(buf, ph, p, way, 1, "start", True, "end")
        for s in range(min(NEAR, ncol - 1), 1, -1):
            for way in (0, 1):
                zsend(buf, ph, p, way, s, "start", True)

    def znear(buf, ph, p):
        for way in (0, 1):
            zsend(buf, ph, p, way, 1, "start", True, "middle")

    def arrive(buf, ph, p, s, passes):
        for way in (0, 1):
            sign = 1 - 2 * way
            block = z - sign * s

            @pl.when((block >= 0) & (block <= ncol - 1))
            def _():
                remote(buf.at[block, part(p)], zs.at[ph, p, way, s - 1], zr.at[ph, p, way, s - 1],
                       (r, z - sign)).wait_recv()
            if passes:
                zsend(buf, ph, p, way, s + 1, "start", False)

    def colcopy(it, p, d, owner, device):
        return remote(cols.at[it, rows_of(owner, p)], cs.at[it, p, d], cr.at[it, p, d], (device, z))

    def sibcopy(it, p, d, owner):
        return remote(cols.at[it, rows_of(owner, p)], ss.at[it, p, d], sr.at[it, p, d], (sib, z))

    def chunk(buf, it, p, j, fresh):
        rows = pl.ds(pl.multiple_of(j * w, w), w)
        if fresh:
            bhigh, blow = split(cols[it, rows, :])
            bh[rows, :] = bhigh
            bl[rows, :] = blow
        else:
            bhigh, blow = bh[rows, :], bl[rows, :]
        ahigh, alow = split(buf[j, part(p), :])
        both = jnp.concatenate([ahigh, alow], axis=0)
        prod = jnp.dot(both, bhigh, preferred_element_type=jnp.float32)
        rest = jnp.dot(ahigh, blow, preferred_element_type=jnp.float32)
        acc[part(p), :] += prod[:hp] + (prod[hp:] + rest)

    def compute(buf, it, p, s, fresh):
        @pl.when(z - s >= 0)
        def _():
            chunk(buf, it, p, z - s, fresh)

        @pl.when(z + s <= ncol - 1)
        def _():
            chunk(buf, it, p, z + s, fresh)

    def finish(buf, ph, it, p, fresh):
        for s in range(1, min(NEAR, ncol - 1) + 1):
            if s < NEAR:
                arrive(buf, ph, p, s, False)
            compute(buf, it, p, s, fresh)

        def far(s):
            arrive(buf, ph, p, s, True)
            compute(buf, it, p, s, fresh)

        over(NEAR + 1, ncol, far)

    def begin(it, p):
        zown(rowp.at[it], 2 * it, p)
        for d in range(1, plane):
            colcopy(it, p, d, r, flip(chip, d) * 2 + core).start()
        sibcopy(it, p, 0, r).start()

    for p in range(PIECES):
        begin(0, p)
    for p in range(PIECES):
        znear(rowp.at[0], 0, p)
    for it in range(ITERS):
        cur, sq = rowp.at[it], srow.at[it]
        pa, pb = 2 * it, 2 * it + 1
        for p in range(PIECES):
            arrive(cur, pa, p, NEAR, True)
            for d in range(1, plane):
                peer = flip(chip, d) * 2 + core
                colcopy(it, p, d, peer, peer).wait_recv()
                sibcopy(it, p, d, peer).start()
        for p in range(PIECES):
            for d in range(plane):
                sibcopy(it, p, d, flip(chip, d) * 2 + 1 - core).wait_recv()
        for p in range(PIECES):
            chunk(cur, it, p, z, p == 0)
            finish(cur, pa, it, p, p == 0)
            sq[z, part(p), :] = acc[part(p), :] * mask[part(p), :]
            acc[part(p), :] = jnp.zeros((hp, w), jnp.float32)
            zown(sq, pb, p)
        for p in range(PIECES):
            znear(sq, pb, p)
        for p in range(PIECES):
            chunk(sq, it, p, z, False)
            arrive(sq, pb, p, NEAR, True)
        for p in range(PIECES):
            finish(sq, pb, it, p, False)
            result = 3.0 * sq[z, part(p), :] - 2.0 * (mask[part(p), :] * acc[part(p), :])
            if it + 1 < ITERS:
                acc[part(p), :] = jnp.zeros((hp, w), jnp.float32)
                rowp[it + 1, z, part(p), :] = result
                cols[it + 1, rows_of(r, p), :] = result
                begin(it + 1, p)
            else:
                out_ref[part(p), :] = result
        if it + 1 < ITERS:
            for p in range(PIECES):
                znear(rowp.at[it + 1], pa + 2, p)

    for it in range(ITERS):
        for p in range(PIECES):
            for buf, ph in ((rowp.at[it], 2 * it), (srow.at[it], 2 * it + 1)):
                for s in range(1, min(NEAR, ncol - 1) + 1):
                    for way in (0, 1):
                        zsend(buf, ph, p, way, s, "wait", True)

                def sent(s):
                    for way in (0, 1):
                        zsend(buf, ph, p, way, s, "wait", False)

                over(NEAR + 1, ncol, sent)
            for d in range(plane):
                peer = flip(chip, d) * 2 + core
                if d:
                    colcopy(it, p, d, r, peer).wait_send()
                sibcopy(it, p, d, peer).wait_send()


def solution(mesh):
    nrow, ncol = mesh.shape["row"], mesh.shape["col"]

    def per_device(density, pattern):
        h, w = density.shape
        n = nrow * h
        f32 = jnp.float32
        dma = pltpu.SemaphoreType.DMA
        return pl.pallas_call(
            functools.partial(kernel, nrow, ncol),
            out_shape=jax.ShapeDtypeStruct((h, w), f32),
            in_specs=[pl.BlockSpec(memory_space=pltpu.HBM), pl.BlockSpec(memory_space=pltpu.HBM)],
            out_specs=pl.BlockSpec(memory_space=pltpu.VMEM),
            scratch_shapes=[
                pltpu.SMEM(pattern.shape, jnp.int32),
                dma((2,)),
                pltpu.VMEM((ITERS, ncol, h, w), f32),
                pltpu.VMEM((ITERS, n, w), f32),
                pltpu.VMEM((ITERS, ncol, h, w), f32),
                pltpu.VMEM((n, w), jnp.bfloat16),
                pltpu.VMEM((n, w), jnp.bfloat16),
                pltpu.VMEM((h, w), f32),
                pltpu.VMEM((h, w), f32),
                dma((2 * ITERS, PIECES, 2, ncol)),
                dma((2 * ITERS, PIECES, 2, ncol)),
                dma((ITERS, PIECES, nrow // 2)),
                dma((ITERS, PIECES, nrow // 2)),
                dma((ITERS, PIECES, nrow // 2)),
                dma((ITERS, PIECES, nrow // 2)),
            ],
            compiler_params=pltpu.CompilerParams(
                collective_id=0, has_side_effects=True, vmem_limit_bytes=60 * 1024 * 1024),
            cost_estimate=pl.CostEstimate(
                flops=12 * ITERS * h * n * w, bytes_accessed=8 * h * w, transcendentals=0),
        )(pattern, density)

    return jax.shard_map(
        per_device,
        mesh=mesh,
        in_specs=(P("row", "col"), P("row", "col")),
        out_specs=P("row", "col"),
        check_vma=False,
    )
```

```python
import functools

import jax
import jax.numpy as jnp
from jax import lax
from jax.experimental import pallas as pl
from jax.experimental.pallas import tpu as pltpu
from jax.sharding import PartitionSpec as P

ITERS = 2
PIECES = 2
NEAR = 2
MESH = pl.DeviceIdType.MESH


def split(x):
    high = x.astype(jnp.bfloat16)
    low = (x - high.astype(jnp.float32)).astype(jnp.bfloat16)
    return high, low


def flip(index, mask):
    bit = 1
    while bit <= mask:
        if mask & bit:
            index = index + bit * (1 - 2 * lax.rem(index // bit, 2))
        bit *= 2
    return index


def kernel(nrow, ncol, pattern_hbm, density_ref, out_ref, pattern_ref, local, rowp, cols, srow, bh, bl, acc, mask,
           zs, zr, cs, cr, ss, sr):
    h, w = density_ref.shape
    pr, pc = pattern_hbm.shape
    plane = nrow // 2
    r, z = lax.axis_index("row"), lax.axis_index("col")
    core = lax.rem(r, 2)
    chip = r // 2
    sib = r + 1 - 2 * core
    hp = h // PIECES

    take_pattern = pltpu.make_async_copy(pattern_hbm, pattern_ref, local.at[0])
    take_density = pltpu.make_async_copy(density_ref, rowp.at[0, z], local.at[1])
    take_pattern.start()
    take_density.start()
    barrier = pltpu.get_barrier_semaphore()
    hops = sorted({d % ncol for near in range(1, NEAR + 1) for d in (near, -near)} - {0})
    greet = [(flip(chip, d) * 2 + core, z) for d in range(1, plane)] + [(sib, z)]
    greet += [(r, lax.rem(z + d, ncol)) for d in hops]
    for device in greet:
        pl.semaphore_signal(barrier, inc=1, device_id=device, device_id_type=MESH)

    take_pattern.wait()
    lane_block = lax.broadcasted_iota(jnp.int32, (h // pr, w), 1) // (w // pc)
    for i in range(pr):
        band = jnp.zeros((h // pr, w), jnp.float32)
        for j in range(pc):
            band = jnp.where(lane_block == j, pattern_ref[i, j].astype(jnp.float32), band)
        mask[i * (h // pr):(i + 1) * (h // pr), :] = band

    def rows_of(owner, p):
        return pl.ds(pl.multiple_of(owner * h + p * hp, hp), hp)

    def part(p):
        return pl.ds(p * hp, hp)

    take_density.wait()
    cols[0, pl.ds(pl.multiple_of(r * h, h), h), :] = rowp[0, z]
    acc[...] = jnp.zeros_like(acc)
    pl.semaphore_wait(barrier, len(greet))

    def remote(ref, send, recv, device):
        return pltpu.make_async_remote_copy(
            src_ref=ref, dst_ref=ref, send_sem=send, recv_sem=recv, device_id=device, device_id_type=MESH)

    def over(low, high, body):
        if ncol <= 4:
            for s in range(low, high):
                body(s)
        else:
            lax.fori_loop(low, high, lambda s, c: (body(s), c)[1], 0)

    def zsend(buf, ph, p, way, s, act, near, only=None):
        sign = 1 - 2 * way
        back = 0 if near else s - 1
        ahead = s if near else 1
        block, to = z - sign * back, z + sign * ahead

        inside = (block >= 0) & (block <= ncol - 1) & (to >= 0) & (to <= ncol - 1)
        if only == "end":
            inside = (to == (ncol - 1 if way == 0 else 0)) & (block >= 0) & (block <= ncol - 1)
        elif only == "middle":
            inside = (to > 0) & (to < ncol - 1)

        @pl.when(inside)
        def _():
            copy = remote(buf.at[block, part(p)], zs.at[ph, p, way, s - 1], zr.at[ph, p, way, s - 1], (r, to))
            copy.start() if act == "start" else copy.wait_send()

    def zown(buf, ph, p):
        for way in (0, 1):
            zsend(buf, ph, p, way, 1, "start", True, "end")
        for s in range(min(NEAR, ncol - 1), 1, -1):
            for way in (0, 1):
                zsend(buf, ph, p, way, s, "start", True)

    def znear(buf, ph, p):
        for way in (0, 1):
            zsend(buf, ph, p, way, 1, "start", True, "middle")

    def arrive(buf, ph, p, s, passes):
        for way in (0, 1):
            sign = 1 - 2 * way
            block = z - sign * s

            @pl.when((block >= 0) & (block <= ncol - 1))
            def _():
                remote(buf.at[block, part(p)], zs.at[ph, p, way, s - 1], zr.at[ph, p, way, s - 1],
                       (r, z - sign)).wait_recv()
            if passes:
                zsend(buf, ph, p, way, s + 1, "start", False)

    def colcopy(it, p, d, owner, device):
        return remote(cols.at[it, rows_of(owner, p)], cs.at[it, p, d], cr.at[it, p, d], (device, z))

    def sibcopy(it, p, d, owner):
        return remote(cols.at[it, rows_of(owner, p)], ss.at[it, p, d], sr.at[it, p, d], (sib, z))

    def chunk(buf, it, p, j, fresh):
        rows = pl.ds(pl.multiple_of(j * w, w), w)
        if fresh:
            bhigh, blow = split(cols[it, rows, :])
            bh[rows, :] = bhigh
            bl[rows, :] = blow
        else:
            bhigh, blow = bh[rows, :], bl[rows, :]
        ahigh, alow = split(buf[j, part(p), :])
        both = jnp.concatenate([ahigh, alow], axis=0)
        prod = jnp.dot(both, bhigh, preferred_element_type=jnp.float32)
        rest = jnp.dot(ahigh, blow, preferred_element_type=jnp.float32)
        acc[part(p), :] += prod[:hp] + (prod[hp:] + rest)

    def compute(buf, it, p, s, fresh):
        @pl.when(z - s >= 0)
        def _():
            chunk(buf, it, p, z - s, fresh)

        @pl.when(z + s <= ncol - 1)
        def _():
            chunk(buf, it, p, z + s, fresh)

    def finish(buf, ph, it, p, fresh):
        for s in range(1, min(NEAR, ncol - 1) + 1):
            if s < NEAR:
                arrive(buf, ph, p, s, False)
            compute(buf, it, p, s, fresh)

        def far(s):
            arrive(buf, ph, p, s, True)
            compute(buf, it, p, s, fresh)

        over(NEAR + 1, ncol, far)

    def begin(it, p):
        if it:
            zown(rowp.at[it], 2 * it, p)
        for d in range(1, plane):
            colcopy(it, p, d, r, flip(chip, d) * 2 + core).start()
        sibcopy(it, p, 0, r).start()

    for p in range(PIECES):
        zown(rowp.at[0], 0, p)
    for p in range(PIECES):
        begin(0, p)
    for p in range(PIECES):
        znear(rowp.at[0], 0, p)
    for it in range(ITERS):
        cur, sq = rowp.at[it], srow.at[it]
        pa, pb = 2 * it, 2 * it + 1
        for p in range(PIECES):
            arrive(cur, pa, p, NEAR, True)
            for d in range(1, plane):
                peer = flip(chip, d) * 2 + core
                colcopy(it, p, d, peer, peer).wait_recv()
                sibcopy(it, p, d, peer).start()
        for p in range(PIECES):
            for d in range(plane):
                sibcopy(it, p, d, flip(chip, d) * 2 + 1 - core).wait_recv()
        for p in range(PIECES):
            chunk(cur, it, p, z, p == 0)
            finish(cur, pa, it, p, p == 0)
            sq[z, part(p), :] = acc[part(p), :] * mask[part(p), :]
            acc[part(p), :] = jnp.zeros((hp, w), jnp.float32)
            zown(sq, pb, p)
        for p in range(PIECES):
            znear(sq, pb, p)
        for p in range(PIECES):
            chunk(sq, it, p, z, False)
            arrive(sq, pb, p, NEAR, True)
        for p in range(PIECES):
            finish(sq, pb, it, p, False)
            result = 3.0 * sq[z, part(p), :] - 2.0 * (mask[part(p), :] * acc[part(p), :])
            if it + 1 < ITERS:
                acc[part(p), :] = jnp.zeros((hp, w), jnp.float32)
                rowp[it + 1, z, part(p), :] = result
                cols[it + 1, rows_of(r, p), :] = result
                begin(it + 1, p)
            else:
                out_ref[part(p), :] = result
        if it + 1 < ITERS:
            for p in range(PIECES):
                znear(rowp.at[it + 1], pa + 2, p)

    for it in range(ITERS):
        for p in range(PIECES):
            for buf, ph in ((rowp.at[it], 2 * it), (srow.at[it], 2 * it + 1)):
                for s in range(1, min(NEAR, ncol - 1) + 1):
                    for way in (0, 1):
                        zsend(buf, ph, p, way, s, "wait", True)

                def sent(s):
                    for way in (0, 1):
                        zsend(buf, ph, p, way, s, "wait", False)

                over(NEAR + 1, ncol, sent)
            for d in range(plane):
                peer = flip(chip, d) * 2 + core
                if d:
                    colcopy(it, p, d, r, peer).wait_send()
                sibcopy(it, p, d, peer).wait_send()


def solution(mesh):
    nrow, ncol = mesh.shape["row"], mesh.shape["col"]

    def per_device(density, pattern):
        h, w = density.shape
        n = nrow * h
        f32 = jnp.float32
        dma = pltpu.SemaphoreType.DMA
        return pl.pallas_call(
            functools.partial(kernel, nrow, ncol),
            out_shape=jax.ShapeDtypeStruct((h, w), f32),
            in_specs=[pl.BlockSpec(memory_space=pltpu.HBM), pl.BlockSpec(memory_space=pltpu.HBM)],
            out_specs=pl.BlockSpec(memory_space=pltpu.VMEM),
            scratch_shapes=[
                pltpu.SMEM(pattern.shape, jnp.int32),
                dma((2,)),
                pltpu.VMEM((ITERS, ncol, h, w), f32),
                pltpu.VMEM((ITERS, n, w), f32),
                pltpu.VMEM((ITERS, ncol, h, w), f32),
                pltpu.VMEM((n, w), jnp.bfloat16),
                pltpu.VMEM((n, w), jnp.bfloat16),
                pltpu.VMEM((h, w), f32),
                pltpu.VMEM((h, w), f32),
                dma((2 * ITERS, PIECES, 2, ncol)),
                dma((2 * ITERS, PIECES, 2, ncol)),
                dma((ITERS, PIECES, nrow // 2)),
                dma((ITERS, PIECES, nrow // 2)),
                dma((ITERS, PIECES, nrow // 2)),
                dma((ITERS, PIECES, nrow // 2)),
            ],
            compiler_params=pltpu.CompilerParams(
                collective_id=0, has_side_effects=True, vmem_limit_bytes=60 * 1024 * 1024),
            cost_estimate=pl.CostEstimate(
                flops=12 * ITERS * h * n * w, bytes_accessed=8 * h * w, transcendentals=0),
        )(pattern, density)

    return jax.shard_map(
        per_device,
        mesh=mesh,
        in_specs=(P("row", "col"), P("row", "col")),
        out_specs=P("row", "col"),
        check_vma=False,
    )
```
